512 devices in a mesh: wide: 64 (over z, x, y_lo), narrow: 8 (over y_hi, core).
Axes of the slice: x: 4, y: 8 (y_hi: 4, y_lo: 2; y = y_hi * 2 + y_lo), z: 8, core: 2. Of those that a mesh axis runs over, the one named last changes fastest.
Arguments:
- layer_input: bfloat16 [512, 8192], P('wide', 'narrow'), may hold values from -6 to 6
- up_weight: bfloat16 [8192, 32768], P('narrow', 'wide'), may hold values from -0.0625 to 0.0625
- up_bias: float32 [32768], P('wide'), may hold values from -4 to 4
- down_weight: bfloat16 [32768, 8192], P('wide', 'narrow'), may hold values from -0.03125 to 0.03125
- grad_output: bfloat16 [512, 8192], P('wide', 'narrow'), may hold values from -6 to 6
Outputs:
- input_grad: bfloat16 [512, 8192], P('wide', 'narrow')
- up_grad: bfloat16 [8192, 32768], P('narrow', 'wide')
- bias_grad: float32 [32768], P('wide')
- down_grad: bfloat16 [32768, 8192], P('wide', 'narrow')
The draws below stay inside these ranges and needn't reach their ends.
All inputs are finite; a program needn't handle non-finite values.
Results may differ from the reference program's by a relative error of at most 0.007.
Values may be sent and summed in bfloat16 or wider, within the bound.
No kernel may reach another device: no remote copies, remote signals or barrier semaphores. Data moves between devices by JAX's collectives and lax.ppermute only.
A program may use at most 64 MiB of HBM per device.

```python
import math
import jax
import jax.numpy as jnp
from jax import lax

D = 8192
FF = 32768
TOKENS = 512


def steps_of(rng, extent, split, least, largest):
    def one(axis_at, shards_of):
        steps = jax.random.uniform(jax.random.fold_in(jax.random.fold_in(rng, 6), axis_at), (shards_of,), jnp.float32, least / len(split), largest / len(split))
        return jnp.repeat(jnp.exp(steps), extent[axis_at] // shards_of).reshape((-1,) + (1,) * (len(extent) - axis_at - 1))

    loudness = one(*split[0])
    for cut in split[1:]:
        loudness = loudness * one(*cut)
    return loudness


def normal_values(own_key, dims, scale, most, cuts=(), held_as=jnp.bfloat16):
    entries = scale * jax.random.normal(own_key, dims, jnp.float32)
    if cuts:
        entries = entries * steps_of(own_key, dims, cuts, -0.22, 0.18)
    return jnp.clip(entries, -most, most).astype(held_as)


def setup_inputs(seed: int = 0) -> dict:
    seeds = jax.random.split(jax.random.key(seed), 6)
    return {
        "layer_input": normal_values(seeds[0], (TOKENS, D), 1.0, 6.0, ((0, 64), (1, 8))),
        "up_weight": normal_values(seeds[1], (D, FF), D ** -0.5, 0.0625, ((0, 8), (1, 64))),
        "up_bias": normal_values(seeds[2], (FF,), 1.0, 4.0, ((0, 64),), jnp.float32),
        "down_weight": normal_values(seeds[3], (FF, D), FF ** -0.5, 0.03125, ((0, 64), (1, 8))),
        "grad_output": normal_values(seeds[4], (TOKENS, D), 1.0, 6.0, ((0, 64), (1, 8))),
    }


root_coef = 0.7978845608
cube_coef = 0.044715

def gelu_value(pre):
    inner = jnp.tanh(root_coef * (pre + cube_coef * pre * pre * pre))
    return 0.5 * pre * (1.0 + inner)

def gelu_slope(pre):
    inner = jnp.tanh(root_coef * (pre + cube_coef * pre * pre * pre))
    return 0.5 * (1.0 + inner) + 0.5 * pre * (1.0 - inner * inner) * root_coef * (1.0 + 3.0 * cube_coef * pre * pre)

def reference(layer_input, up_weight, up_bias, down_weight, grad_output):
    factor = 1.0 / math.sqrt(TOKENS)
    pre = jnp.dot(layer_input, up_weight, preferred_element_type=jnp.float32) + up_bias[None, :]
    activ = gelu_value(pre).astype(jnp.bfloat16)
    back = lax.dot_general(grad_output, down_weight, (((1,), (1,)), ((), ())), preferred_element_type=jnp.float32)
    d_pre = (back * gelu_slope(pre)).astype(jnp.bfloat16)
    input_grad = lax.dot_general(d_pre, up_weight, (((1,), (1,)), ((), ())), preferred_element_type=jnp.float32).astype(jnp.bfloat16)
    up_grad = (lax.dot_general(layer_input, d_pre, (((0,), (0,)), ((), ())), preferred_element_type=jnp.float32) * factor).astype(jnp.bfloat16)
    down_grad = (lax.dot_general(activ, grad_output, (((0,), (0,)), ((), ())), preferred_element_type=jnp.float32) * factor).astype(jnp.bfloat16)
    bias_grad = lax.optimization_barrier(jnp.sum(d_pre, axis=0, dtype=jnp.float32)) * factor
    return (input_grad, up_grad, bias_grad, down_grad)
```

```python
import functools
import math

import jax
import jax.numpy as jnp
from jax import lax
from jax.experimental import pallas as pl
from jax.experimental.pallas import tpu as pltpu
from jax.sharding import Mesh, PartitionSpec as P

AXES = ("z", "x", "yl", "yh", "core")
SIZES = (8, 4, 2, 4, 2)
NEAR = ("x", "yl")
WIDE = ("z", "x", "yl")
NARROW = ("yh", "core")

root_coef = 0.7978845608
cube_coef = 0.044715
f32 = jnp.float32
bf16 = jnp.bfloat16
VMEM = 40 * 1024 * 1024


def cost(flops, moved):
    return pl.CostEstimate(flops=flops, bytes_accessed=moved, transcendentals=0)


def forward_kernel(core_ref, x_ref, g_ref, up_ref, down_ref, send_ref, keep_ref):
    hidden = up_ref.shape[1]
    pre = jnp.dot(x_ref[...], up_ref[...], preferred_element_type=f32)
    back = lax.dot_general(
        g_ref[...], down_ref[...], (((1,), (1,)), ((), ())), preferred_element_type=f32
    )

    @pl.when(pl.program_id(0) < 2)
    def _():
        send_ref[:, :hidden] = pre.astype(bf16)
        send_ref[:, hidden:] = back.astype(bf16)

    @pl.when(pl.program_id(0) >= 2)
    def _():
        keep_ref[:, :hidden] = pre
        keep_ref[:, hidden:] = back


def forward(core, both, up_weight, down_weight):
    tokens, width = both.shape[0], both.shape[1] // 2
    hidden = up_weight.shape[1]
    rows = tokens // 4

    def block_of(i, c):
        return jnp.where(i < 2, (1 - c[0]) * 2 + i, c[0] * 2 + i - 2)

    return pl.pallas_call(
        forward_kernel,
        grid_spec=pltpu.PrefetchScalarGridSpec(
            num_scalar_prefetch=1,
            grid=(4,),
            in_specs=[
                pl.BlockSpec((rows, width), lambda i, c: (block_of(i, c), 0)),
                pl.BlockSpec((rows, width), lambda i, c: (block_of(i, c), 1)),
                pl.BlockSpec((width, hidden), lambda i, c: (0, 0)),
                pl.BlockSpec((hidden, width), lambda i, c: (0, 0)),
            ],
            out_specs=[
                pl.BlockSpec((rows, 2 * hidden), lambda i, c: (jnp.minimum(i, 1), 0)),
                pl.BlockSpec((rows, 2 * hidden), lambda i, c: (jnp.maximum(i - 2, 0), 0)),
            ],
        ),
        out_shape=[
            jax.ShapeDtypeStruct((2 * rows, 2 * hidden), bf16),
            jax.ShapeDtypeStruct((2 * rows, 2 * hidden), f32),
        ],
        compiler_params=pltpu.CompilerParams(vmem_limit_bytes=VMEM),
        cost_estimate=cost(4 * tokens * width * hidden, 4 * (tokens * width + width * hidden)),
        name="forward_products",
    )(core, both, both, up_weight, down_weight)


def activate_kernel(parts_ref, bias_ref, out_ref):
    hidden = bias_ref.shape[1]
    total = parts_ref[0].astype(f32)
    for k in range(1, parts_ref.shape[0]):
        total = total + parts_ref[k].astype(f32)
    pre = total[:, :hidden] + bias_ref[...]
    back = total[:, hidden:]
    square = pre * pre
    inner = jnp.tanh(root_coef * (pre + cube_coef * square * pre))
    half = 0.5 * (1.0 + inner)
    activ = (pre * half).astype(bf16)
    slope = half + 0.5 * pre * (1.0 - inner * inner) * root_coef * (
        1.0 + 3.0 * cube_coef * square
    )
    d_pre = (back * slope).astype(bf16)
    for k in range(out_ref.shape[0]):
        out_ref[k, :, :hidden] = d_pre
        out_ref[k, :, hidden:] = activ


def activate(parts, up_bias):
    return pl.pallas_call(
        activate_kernel,
        out_shape=jax.ShapeDtypeStruct(parts.shape, bf16),
        compiler_params=pltpu.CompilerParams(vmem_limit_bytes=VMEM),
        cost_estimate=cost(32 * parts.size, 4 * parts.size),
        name="activate",
    )(parts, up_bias)


def input_kernel(core_ref, own_ref, other_ref, up_ref, out_ref):
    def product(ref):
        out_ref[...] = lax.dot_general(
            ref[...], up_ref[...], (((1,), (1,)), ((), ())), preferred_element_type=f32
        ).astype(bf16)

    @pl.when(pl.program_id(0) < 2)
    def _():
        product(own_ref)

    @pl.when(pl.program_id(0) >= 2)
    def _():
        product(other_ref)


def input_product(core, own, other, up_weight):
    width, hidden = up_weight.shape
    rows = own.shape[0] // 2
    return pl.pallas_call(
        input_kernel,
        grid_spec=pltpu.PrefetchScalarGridSpec(
            num_scalar_prefetch=1,
            grid=(4,),
            in_specs=[
                pl.BlockSpec((rows, hidden), lambda i, c: (jnp.minimum(i, 1), 0)),
                pl.BlockSpec((rows, hidden), lambda i, c: (jnp.maximum(i - 2, 0), 0)),
                pl.BlockSpec((width, hidden), lambda i, c: (0, 0)),
            ],
            out_specs=pl.BlockSpec(
                (rows, width),
                lambda i, c: (jnp.where(i < 2, c[0] * 2 + i, (1 - c[0]) * 2 + i - 2), 0),
            ),
        ),
        out_shape=jax.ShapeDtypeStruct((4 * rows, width), bf16),
        compiler_params=pltpu.CompilerParams(vmem_limit_bytes=VMEM),
        cost_estimate=cost(8 * rows * width * hidden, 2 * width * (4 * rows + hidden)),
        name="input_product",
    )(core, own, other, up_weight)


def weights_kernel(
    factor, core_ref, x0_ref, x1_ref, g0_ref, g1_ref, own_ref, other_ref, up_ref, bias_ref, down_ref
):
    hidden = up_ref.shape[1]

    def across(a, b):
        return lax.dot_general(a, b, (((0,), (0,)), ((), ())), preferred_element_type=f32)

    up = across(x0_ref[...], own_ref[:, :hidden]) + across(x1_ref[...], other_ref[:, :hidden])
    up_ref[...] = (up * factor).astype(bf16)
    down = across(own_ref[:, hidden:], g0_ref[...]) + across(other_ref[:, hidden:], g1_ref[...])
    down_ref[...] = (down * factor).astype(bf16)

    @pl.when(pl.program_id(0) == 0)
    def _():
        own = jnp.sum(own_ref[:, :hidden].astype(f32), axis=0, keepdims=True)
        other = jnp.sum(other_ref[:, :hidden].astype(f32), axis=0, keepdims=True)
        bias_ref[...] = (own + other) * factor


def weights_product(factor, core, both, own, other):
    tokens, width = both.shape[0], both.shape[1] // 2
    hidden = own.shape[1] // 2
    steps = 4
    cols = width // steps
    half = tokens // 2

    def spec(mine, at):
        return pl.BlockSpec(
            (half, cols), lambda i, c: (c[0] if mine else 1 - c[0], i + at * steps)
        )

    whole = pl.BlockSpec((half, 2 * hidden), lambda i, c: (0, 0))
    return pl.pallas_call(
        functools.partial(weights_kernel, factor),
        grid_spec=pltpu.PrefetchScalarGridSpec(
            num_scalar_prefetch=1,
            grid=(steps,),
            in_specs=[spec(True, 0), spec(False, 0), spec(True, 1), spec(False, 1), whole, whole],
            out_specs=[
                pl.BlockSpec((cols, hidden), lambda i, c: (i, 0)),
                pl.BlockSpec((1, hidden), lambda i, c: (0, 0)),
                pl.BlockSpec((hidden, cols), lambda i, c: (0, i)),
            ],
        ),
        out_shape=[
            jax.ShapeDtypeStruct((width, hidden), bf16),
            jax.ShapeDtypeStruct((1, hidden), f32),
            jax.ShapeDtypeStruct((hidden, width), bf16),
        ],
        compiler_params=pltpu.CompilerParams(vmem_limit_bytes=VMEM),
        cost_estimate=cost(4 * tokens * width * hidden, 4 * (tokens * width + width * hidden)),
        name="weights_product",
    )(core, both, both, both, both, own, other)


def spread(block, axes):
    copies = jnp.broadcast_to(block[None], (lax.axis_size(axes),) + block.shape)
    return lax.all_to_all(copies, axes, 0, 0)


def collect(parts, axes):
    count = lax.axis_size(axes)
    parts = parts.reshape((count, parts.shape[0] // count) + parts.shape[1:])
    return jnp.sum(lax.all_to_all(parts, axes, 0, 0).astype(f32), axis=0).astype(bf16)


def swap(block):
    return lax.ppermute(block, "core", [(0, 1), (1, 0)])


def shards(layer_input, up_weight, up_bias, down_weight, grad_output):
    tokens_here, width = layer_input.shape
    hidden = up_weight.shape[1]
    tokens = tokens_here * lax.axis_size(WIDE)
    factor = 1.0 / math.sqrt(tokens)
    core = lax.axis_index("core").astype(jnp.int32)[None]

    both = jnp.concatenate([layer_input, grad_output], axis=1)
    both = spread(both, "z").reshape(-1, 2 * width)
    both = spread(both, NEAR).reshape(-1, 2 * width)

    send, keep = forward(core, both, up_weight, down_weight)
    chip = (keep + swap(send).astype(f32)).astype(bf16)
    quarters = lax.axis_size("yh")
    chip = chip.reshape(quarters, -1, 2 * hidden)
    parts = lax.all_to_all(chip, "yh", 0, 0)
    own = lax.all_to_all(activate(parts, up_bias[None]), "yh", 0, 0).reshape(-1, 2 * hidden)
    other = swap(own)

    partial = input_product(core, own, other, up_weight)
    input_grad = collect(collect(partial, NEAR), "z")
    up_grad, bias_grad, down_grad = weights_product(factor, core, both, own, other)
    return (input_grad, up_grad, bias_grad[0], down_grad)


def solution(mesh):
    fine = Mesh(mesh.devices.reshape(SIZES), AXES)
    in_specs = (
        P(WIDE, NARROW),
        P(NARROW, WIDE),
        P(WIDE),
        P(WIDE, NARROW),
        P(WIDE, NARROW),
    )
    out_specs = (P(WIDE, NARROW), P(NARROW, WIDE), P(WIDE), P(WIDE, NARROW))
    return jax.shard_map(shards, mesh=fine, in_specs=in_specs, out_specs=out_specs, check_vma=False)
```

```python
import functools
import math

import jax
import jax.numpy as jnp
from jax import lax
from jax.experimental import pallas as pl
from jax.experimental.pallas import tpu as pltpu
from jax.sharding import Mesh, PartitionSpec as P

AXES = ("z", "x", "yl", "yh", "core")
SIZES = (8, 4, 2, 4, 2)
NEAR = ("x", "yl")
WIDE = ("z", "x", "yl")
NARROW = ("yh", "core")

root_coef = 0.7978845608
cube_coef = 0.044715
f32 = jnp.float32
bf16 = jnp.bfloat16
VMEM = 16 * 1024 * 1024


def cost(flops, moved):
    return pl.CostEstimate(flops=flops, bytes_accessed=moved, transcendentals=0)


def forward_kernel(core_ref, x_ref, g_ref, up_ref, down_ref, send_ref, keep_ref):
    hidden = up_ref.shape[1]
    pre = jnp.dot(x_ref[...], up_ref[...], preferred_element_type=f32)
    back = lax.dot_general(
        g_ref[...], down_ref[...], (((1,), (1,)), ((), ())), preferred_element_type=f32
    )

    @pl.when(pl.program_id(0) == 0)
    def _():
        send_ref[:, :hidden] = pre.astype(bf16)
        send_ref[:, hidden:] = back.astype(bf16)

    @pl.when(pl.program_id(0) == 1)
    def _():
        keep_ref[:, :hidden] = pre
        keep_ref[:, hidden:] = back


def forward(core, both, up_weight, down_weight):
    tokens, width = both.shape[0], both.shape[1] // 2
    hidden = up_weight.shape[1]
    rows = tokens // 2

    def rows_of(at):
        return pl.BlockSpec((rows, width), lambda i, c: (jnp.where(i == 0, 1 - c[0], c[0]), at))

    return pl.pallas_call(
        forward_kernel,
        grid_spec=pltpu.PrefetchScalarGridSpec(
            num_scalar_prefetch=1,
            grid=(2,),
            in_specs=[
                rows_of(0),
                rows_of(1),
                pl.BlockSpec((width, hidden), lambda i, c: (0, 0)),
                pl.BlockSpec((hidden, width), lambda i, c: (0, 0)),
            ],
            out_specs=[pl.BlockSpec((rows, 2 * hidden), lambda i, c: (0, 0))] * 2,
        ),
        out_shape=[
            jax.ShapeDtypeStruct((rows, 2 * hidden), bf16),
            jax.ShapeDtypeStruct((rows, 2 * hidden), f32),
        ],
        compiler_params=pltpu.CompilerParams(vmem_limit_bytes=VMEM),
        cost_estimate=cost(4 * tokens * width * hidden, 4 * (tokens * width + width * hidden)),
        name="forward_products",
    )(core, both, both, up_weight, down_weight)


def activate_kernel(parts_ref, bias_ref, d_pre_ref, activ_ref):
    hidden = bias_ref.shape[1]
    total = parts_ref[0].astype(f32)
    for k in range(1, parts_ref.shape[0]):
        total = total + parts_ref[k].astype(f32)
    pre = total[:, :hidden] + bias_ref[...]
    back = total[:, hidden:]
    square = pre * pre
    inner = jnp.tanh(root_coef * (pre + cube_coef * square * pre))
    half = 0.5 * (1.0 + inner)
    slope = half + 0.5 * pre * (1.0 - inner * inner) * root_coef * (
        1.0 + 3.0 * cube_coef * square
    )
    activ_ref[...] = (pre * half).astype(bf16)
    d_pre = (back * slope).astype(bf16)
    for k in range(d_pre_ref.shape[0]):
        d_pre_ref[k] = d_pre


def activate(parts, up_bias):
    quarters, rows, hidden = parts.shape[0], parts.shape[1], parts.shape[2] // 2
    return pl.pallas_call(
        activate_kernel,
        out_shape=[
            jax.ShapeDtypeStruct((quarters, rows, hidden), bf16),
            jax.ShapeDtypeStruct((rows, hidden), bf16),
        ],
        compiler_params=pltpu.CompilerParams(vmem_limit_bytes=VMEM),
        cost_estimate=cost(32 * parts.size, 4 * parts.size),
        name="activate",
    )(parts, up_bias)


def input_kernel(d_ref, up_ref, out_ref):
    out_ref[...] = lax.dot_general(
        d_ref[...], up_ref[...], (((1,), (1,)), ((), ())), preferred_element_type=f32
    ).astype(bf16)


def input_product(d_pre, up_weight):
    width, hidden = up_weight.shape
    steps = 2
    rows = d_pre.shape[0] // steps
    return pl.pallas_call(
        input_kernel,
        grid=(steps,),
        in_specs=[
            pl.BlockSpec((rows, hidden), lambda i: (i, 0)),
            pl.BlockSpec((width, hidden), lambda i: (0, 0)),
        ],
        out_specs=pl.BlockSpec((rows, width), lambda i: (i, 0)),
        out_shape=jax.ShapeDtypeStruct((steps * rows, width), bf16),
        compiler_params=pltpu.CompilerParams(vmem_limit_bytes=VMEM),
        cost_estimate=cost(2 * steps * rows * width * hidden, 2 * width * (steps * rows + hidden)),
        name="input_product",
    )(d_pre, up_weight)


def across(a, b):
    return lax.dot_general(a, b, (((0,), (0,)), ((), ())), preferred_element_type=f32)


def up_kernel(factor, x_ref, d_ref, up_ref, bias_ref):
    up_ref[...] = (across(x_ref[...], d_ref[...]) * factor).astype(bf16)

    @pl.when(pl.program_id(0) == 0)
    def _():
        bias_ref[...] = jnp.sum(d_ref[...].astype(f32), axis=0, keepdims=True) * factor


def up_product(factor, both, d_pre):
    tokens, width = both.shape[0], both.shape[1] // 2
    hidden = d_pre.shape[1]
    steps = 4
    cols = width // steps
    return pl.pallas_call(
        functools.partial(up_kernel, factor),
        grid=(steps,),
        in_specs=[
            pl.BlockSpec((tokens, cols), lambda i: (0, i)),
            pl.BlockSpec((tokens, hidden), lambda i: (0, 0)),
        ],
        out_specs=[
            pl.BlockSpec((cols, hidden), lambda i: (i, 0)),
            pl.BlockSpec((1, hidden), lambda i: (0, 0)),
        ],
        out_shape=[
            jax.ShapeDtypeStruct((width, hidden), bf16),
            jax.ShapeDtypeStruct((1, hidden), f32),
        ],
        compiler_params=pltpu.CompilerParams(vmem_limit_bytes=VMEM),
        cost_estimate=cost(2 * tokens * width * hidden, 2 * (tokens * width + width * hidden)),
        name="up_product",
    )(both, d_pre)


def down_kernel(factor, quarter_ref, pieces_ref, g_ref, down_ref, activ_ref):
    cores, count, rows = pieces_ref.shape[:3]

    @pl.when(pl.program_id(0) == 0)
    def _():
        for k in range(count):
            sender = lax.rem(quarter_ref[0] - k + count, count)
            for j in range(cores):
                start = pl.multiple_of((j * count + sender) * rows, rows)
                activ_ref[pl.ds(start, rows), :] = pieces_ref[j, k]

    down_ref[...] = (across(activ_ref[...], g_ref[...]) * factor).astype(bf16)


def down_product(factor, quarter, both, pieces):
    tokens, width = both.shape[0], both.shape[1] // 2
    hidden = pieces.shape[-1]
    steps = 4
    cols = width // steps
    return pl.pallas_call(
        functools.partial(down_kernel, factor),
        grid_spec=pltpu.PrefetchScalarGridSpec(
            num_scalar_prefetch=1,
            grid=(steps,),
            in_specs=[
                pl.BlockSpec(pieces.shape, lambda i, c: (0, 0, 0, 0)),
                pl.BlockSpec((tokens, cols), lambda i, c: (0, i + steps)),
            ],
            out_specs=pl.BlockSpec((hidden, cols), lambda i, c: (0, i)),
            scratch_shapes=[pltpu.VMEM((tokens, hidden), bf16)],
        ),
        out_shape=jax.ShapeDtypeStruct((hidden, width), bf16),
        compiler_params=pltpu.CompilerParams(vmem_limit_bytes=VMEM),
        cost_estimate=cost(2 * tokens * width * hidden, 2 * (tokens * width + width * hidden)),
        name="down_product",
    )(quarter, pieces, both)


def spread(block, axes):
    copies = jnp.broadcast_to(block[None], (lax.axis_size(axes),) + block.shape)
    return lax.all_to_all(copies, axes, 0, 0)


def collect(parts, axes):
    count = lax.axis_size(axes)
    parts = parts.reshape((count, parts.shape[0] // count) + parts.shape[1:])
    return jnp.sum(lax.all_to_all(parts, axes, 0, 0).astype(f32), axis=0).astype(bf16)


def swap(block):
    return lax.ppermute(block, "core", [(0, 1), (1, 0)])


def shards(layer_input, up_weight, up_bias, down_weight, grad_output):
    tokens_here, width = layer_input.shape
    hidden = up_weight.shape[1]
    tokens = tokens_here * lax.axis_size(WIDE)
    factor = 1.0 / math.sqrt(tokens)
    core = lax.axis_index("core").astype(jnp.int32)[None]
    quarters = lax.axis_size("yh")

    both = jnp.concatenate([layer_input, grad_output], axis=1)
    both = spread(both, "z").reshape(-1, 2 * width)
    both = spread(both, NEAR).reshape(-1, 2 * width)

    send, keep = forward(core, both, up_weight, down_weight)
    chip = (keep + swap(send).astype(f32)).astype(bf16)
    sums = lax.all_to_all(chip.reshape(quarters, -1, 2 * hidden), "yh", 0, 0)
    copies, activ = activate(sums, up_bias[None])
    own = lax.all_to_all(copies, "yh", 0, 0).reshape(-1, hidden)
    d_pre = lax.all_gather(own, "core", axis=0, tiled=True)
    partial = input_product(d_pre, up_weight)

    partial, activ = lax.optimization_barrier((partial, activ))
    collected = collect(partial, NEAR)
    activs = [activ] + [
        lax.ppermute(activ, "yh", [(i, (i + k) % quarters) for i in range(quarters)])
        for k in range(1, quarters)
    ]
    collected, activs = lax.optimization_barrier((collected, activs))
    up_grad, bias_grad = up_product(factor, both, d_pre)
    quarter = lax.axis_index("yh").astype(jnp.int32)[None]
    activs = lax.all_gather(jnp.stack(activs), "core", axis=0)
    down_grad = down_product(factor, quarter, both, activs)
    input_grad = collect(collected, "z")
    return (input_grad, up_grad, bias_grad[0], down_grad)


def solution(mesh):
    fine = Mesh(mesh.devices.reshape(SIZES), AXES)
    in_specs = (
        P(WIDE, NARROW),
        P(NARROW, WIDE),
        P(WIDE),
        P(WIDE, NARROW),
        P(WIDE, NARROW),
    )
    out_specs = (P(WIDE, NARROW), P(NARROW, WIDE), P(WIDE), P(WIDE, NARROW))
    return jax.shard_map(shards, mesh=fine, in_specs=in_specs, out_specs=out_specs, check_vma=False)
```

```python
import functools
import math

import jax
import jax.numpy as jnp
from jax import lax
from jax.experimental import pallas as pl
from jax.experimental.pallas import tpu as pltpu
from jax.sharding import Mesh, PartitionSpec as P

AXES = ("z", "x", "yl", "yh", "core")
SIZES = (8, 4, 2, 4, 2)
NEAR = ("x", "yl")
WIDE = ("z", "x", "yl")
NARROW = ("yh", "core")

root_coef = 0.7978845608
cube_coef = 0.044715
f32 = jnp.float32
bf16 = jnp.bfloat16
VMEM = 16 * 1024 * 1024


def cost(flops, moved):
    return pl.CostEstimate(flops=flops, bytes_accessed=moved, transcendentals=0)


def in_hbm(array):
    return pltpu.with_memory_space_constraint(array, pltpu.HBM)


def forward_kernel(core_ref, both_ref, up_ref, down_hbm, send_ref, keep_ref, down_ref, sems):
    rows, hidden = send_ref.shape[0], up_ref.shape[1]
    width = up_ref.shape[0]
    fetches = []
    for k in range(sems.shape[0]):
        part = pl.ds(k * (hidden // sems.shape[0]), hidden // sems.shape[0])
        fetches.append(
            pltpu.make_async_copy(down_hbm.at[part], down_ref.at[part], sems.at[k])
        )
        fetches[k].start()
    keep_at = pl.multiple_of(core_ref[0] * rows, rows)
    send_at = pl.multiple_of((1 - core_ref[0]) * rows, rows)

    def pre(start):
        x = both_ref[pl.ds(start, rows), :width]
        return jnp.dot(x, up_ref[...], preferred_element_type=f32)

    def back(start):
        g = both_ref[pl.ds(start, rows), width:]
        return lax.dot_general(
            g, down_ref[...], (((1,), (1,)), ((), ())), preferred_element_type=f32
        )

    send_ref[:, :hidden] = pre(send_at).astype(bf16)
    keep_ref[:, :hidden] = pre(keep_at)
    for fetch in fetches:
        fetch.wait()
    send_ref[:, hidden:] = back(send_at).astype(bf16)
    keep_ref[:, hidden:] = back(keep_at)


def forward(core, both, up_weight, down_weight):
    tokens, width = both.shape[0], both.shape[1] // 2
    hidden = up_weight.shape[1]
    rows = tokens // 2
    vmem = pl.BlockSpec(memory_space=pltpu.VMEM)
    return pl.pallas_call(
        forward_kernel,
        in_specs=[
            pl.BlockSpec(memory_space=pltpu.SMEM),
            vmem,
            vmem,
            pl.BlockSpec(memory_space=pltpu.HBM),
        ],
        out_specs=[vmem, vmem],
        out_shape=[
            jax.ShapeDtypeStruct((rows, 2 * hidden), bf16),
            jax.ShapeDtypeStruct((rows, 2 * hidden), f32),
        ],
        scratch_shapes=[pltpu.VMEM((hidden, width), bf16), pltpu.SemaphoreType.DMA((4,))],
        compiler_params=pltpu.CompilerParams(vmem_limit_bytes=VMEM),
        cost_estimate=cost(4 * tokens * width * hidden, 4 * (tokens * width + width * hidden)),
        name="forward_products",
    )(core, both, up_weight, in_hbm(down_weight))


def activate_kernel(parts_ref, bias_ref, out_ref):
    hidden = bias_ref.shape[1]
    total = parts_ref[0].astype(f32)
    for k in range(1, parts_ref.shape[0]):
        total = total + parts_ref[k].astype(f32)
    pre = total[:, :hidden] + bias_ref[...]
    back = total[:, hidden:]
    square = pre * pre
    inner = jnp.tanh(root_coef * (pre + cube_coef * square * pre))
    half = 0.5 * (1.0 + inner)
    slope = half + 0.5 * pre * (1.0 - inner * inner) * root_coef * (
        1.0 + 3.0 * cube_coef * square
    )
    d_pre = (back * slope).astype(bf16)
    activ = (pre * half).astype(bf16)
    for k in range(out_ref.shape[0]):
        out_ref[k, 0] = d_pre
        out_ref[k, 1] = activ


def activate(parts, up_bias):
    quarters, rows, hidden = parts.shape[0], parts.shape[1], parts.shape[2] // 2
    return pl.pallas_call(
        activate_kernel,
        out_shape=jax.ShapeDtypeStruct((quarters, 2, rows, hidden), bf16),
        compiler_params=pltpu.CompilerParams(vmem_limit_bytes=VMEM),
        cost_estimate=cost(32 * parts.size, 4 * parts.size),
        name="activate",
    )(parts, up_bias)


def input_kernel(d_ref, up_ref, out_ref):
    out_ref[...] = lax.dot_general(
        d_ref[...], up_ref[...], (((1,), (1,)), ((), ())), preferred_element_type=f32
    ).astype(bf16)


def input_product(d_pre, up_weight):
    width, hidden = up_weight.shape
    steps = 2
    rows = d_pre.shape[0] // steps
    return pl.pallas_call(
        input_kernel,
        grid=(steps,),
        in_specs=[
            pl.BlockSpec((rows, hidden), lambda i: (i, 0)),
            pl.BlockSpec((width, hidden), lambda i: (0, 0)),
        ],
        out_specs=pl.BlockSpec((rows, width), lambda i: (i, 0)),
        out_shape=jax.ShapeDtypeStruct((steps * rows, width), bf16),
        compiler_params=pltpu.CompilerParams(vmem_limit_bytes=VMEM),
        cost_estimate=cost(2 * steps * rows * width * hidden, 2 * width * (steps * rows + hidden)),
        name="input_product",
    )(d_pre, up_weight)


def across(a, b):
    return lax.dot_general(a, b, (((0,), (0,)), ((), ())), preferred_element_type=f32)


def weights_kernel(
    factor, both_ref, d_ref, activ_ref, up_hbm, bias_ref, down_hbm, up_ref, down_ref, sems
):
    width, hidden = up_ref.shape
    steps = sems.shape[1]
    copies = []
    for k in range(steps):
        part = pl.ds(k * (width // steps), width // steps)
        up_ref[part, :] = (across(both_ref[:, part], d_ref[...]) * factor).astype(bf16)
        copies.append(pltpu.make_async_copy(up_ref.at[part], up_hbm.at[part], sems.at[0, k]))
        copies[-1].start()
    bias_ref[...] = jnp.sum(d_ref[...].astype(f32), axis=0, keepdims=True) * factor
    for k in range(steps):
        part = pl.ds(k * (hidden // steps), hidden // steps)
        down = across(activ_ref[:, part], both_ref[:, width:])
        down_ref[part, :] = (down * factor).astype(bf16)
        copies.append(pltpu.make_async_copy(down_ref.at[part], down_hbm.at[part], sems.at[1, k]))
        copies[-1].start()
    for copy in copies:
        copy.wait()


def weights_product(factor, both, d_pre, activ):
    tokens, width = both.shape[0], both.shape[1] // 2
    hidden = d_pre.shape[1]
    vmem = pl.BlockSpec(memory_space=pltpu.VMEM)
    hbm = pl.BlockSpec(memory_space=pltpu.HBM)
    return pl.pallas_call(
        functools.partial(weights_kernel, factor),
        in_specs=[vmem] * 3,
        out_specs=[hbm, vmem, hbm],
        out_shape=[
            pltpu.HBM((width, hidden), bf16),
            jax.ShapeDtypeStruct((1, hidden), f32),
            pltpu.HBM((hidden, width), bf16),
        ],
        scratch_shapes=[
            pltpu.VMEM((width, hidden), bf16),
            pltpu.VMEM((hidden, width), bf16),
            pltpu.SemaphoreType.DMA((2, 4)),
        ],
        compiler_params=pltpu.CompilerParams(vmem_limit_bytes=VMEM),
        cost_estimate=cost(4 * tokens * width * hidden, 4 * (tokens * width + width * hidden)),
        name="weights_product",
    )(both, d_pre, activ)


def spread(block, axes):
    copies = jnp.broadcast_to(block[None], (lax.axis_size(axes),) + block.shape)
    return lax.all_to_all(copies, axes, 0, 0)


def swap(block):
    return lax.ppermute(block, "core", [(0, 1), (1, 0)])


def shards(layer_input, up_weight, up_bias, down_weight, grad_output):
    tokens_here, width = layer_input.shape
    hidden = up_weight.shape[1]
    tokens = tokens_here * lax.axis_size(WIDE)
    factor = 1.0 / math.sqrt(tokens)
    core = lax.axis_index("core").astype(jnp.int32)[None]
    quarters = lax.axis_size("yh")

    both = jnp.concatenate([layer_input, grad_output], axis=1)
    both = spread(both, "z").reshape(-1, 2 * width)
    both = spread(both, NEAR).reshape(-1, 2 * width)

    send, keep = forward(core, both, up_weight, down_weight)
    chip = (keep + swap(send).astype(f32)).astype(bf16)
    sums = lax.all_to_all(chip.reshape(quarters, -1, 2 * hidden), "yh", 0, 0)
    copies = activate(sums, up_bias[None])
    own = lax.all_to_all(copies, "yh", 0, 0)
    d_pre = lax.all_gather(own[:, 0].reshape(-1, hidden), "core", axis=0, tiled=True)
    partial = input_product(d_pre, up_weight)
    near = lax.axis_size(NEAR)
    parts = lax.all_to_all(partial.reshape(near, -1, width), NEAR, 0, 0)
    ends = jnp.sum(parts.astype(f32), axis=0).astype(bf16)
    activ = lax.all_gather(own[:, 1].reshape(-1, hidden), "core", axis=0, tiled=True)
    up_grad, bias_grad, down_grad = weights_product(factor, both, d_pre, activ)
    ends = lax.all_to_all(ends.reshape(-1, tokens_here, width), "z", 0, 0)
    input_grad = jnp.sum(ends.astype(f32), axis=0).astype(bf16)
    return (input_grad, up_grad, bias_grad[0], down_grad)


def solution(mesh):
    fine = Mesh(mesh.devices.reshape(SIZES), AXES)
    in_specs = (
        P(WIDE, NARROW),
        P(NARROW, WIDE),
        P(WIDE),
        P(WIDE, NARROW),
        P(WIDE, NARROW),
    )
    out_specs = (P(WIDE, NARROW), P(NARROW, WIDE), P(WIDE), P(WIDE, NARROW))
    return jax.shard_map(shards, mesh=fine, in_specs=in_specs, out_specs=out_specs, check_vma=False)
```

```python
import functools
import math

import jax
import jax.numpy as jnp
from jax import lax
from jax.experimental import pallas as pl
from jax.experimental.pallas import tpu as pltpu
from jax.sharding import Mesh, PartitionSpec as P

AXES = ("z", "x", "yl", "yh", "core")
SIZES = (8, 4, 2, 4, 2)
NEAR = ("x", "yl")
WIDE = ("z", "x", "yl")
NARROW = ("yh", "core")

root_coef = 0.7978845608
cube_coef = 0.044715
f32 = jnp.float32
bf16 = jnp.bfloat16
VMEM = 16 * 1024 * 1024


def cost(flops, moved):
    return pl.CostEstimate(flops=flops, bytes_accessed=moved, transcendentals=0)


def forward_kernel(core_ref, both_ref, up_ref, down_ref, send_ref, keep_ref):
    rows, hidden = send_ref.shape[0], up_ref.shape[1]
    width = up_ref.shape[0]
    keep_at = pl.multiple_of(core_ref[0] * rows, rows)
    send_at = pl.multiple_of((1 - core_ref[0]) * rows, rows)

    def pre(start):
        x = both_ref[pl.ds(start, rows), :width]
        return jnp.dot(x, up_ref[...], preferred_element_type=f32)

    def back(start):
        g = both_ref[pl.ds(start, rows), width:]
        return lax.dot_general(
            g, down_ref[...], (((1,), (1,)), ((), ())), preferred_element_type=f32
        )

    send_ref[:, :hidden] = pre(send_at).astype(bf16)
    send_ref[:, hidden:] = back(send_at).astype(bf16)
    keep_ref[:, :hidden] = pre(keep_at)
    keep_ref[:, hidden:] = back(keep_at)


def forward(core, both, up_weight, down_weight):
    tokens, width = both.shape[0], both.shape[1] // 2
    hidden = up_weight.shape[1]
    rows = tokens // 2
    vmem = pl.BlockSpec(memory_space=pltpu.VMEM)
    return pl.pallas_call(
        forward_kernel,
        in_specs=[pl.BlockSpec(memory_space=pltpu.SMEM), vmem, vmem, vmem],
        out_specs=[vmem, vmem],
        out_shape=[
            jax.ShapeDtypeStruct((rows, 2 * hidden), bf16),
            jax.ShapeDtypeStruct((rows, 2 * hidden), f32),
        ],
        compiler_params=pltpu.CompilerParams(vmem_limit_bytes=VMEM),
        cost_estimate=cost(4 * tokens * width * hidden, 4 * (tokens * width + width * hidden)),
        name="forward_products",
    )(
        core,
        both,
        pltpu.with_memory_space_constraint(up_weight, pltpu.VMEM),
        pltpu.with_memory_space_constraint(down_weight, pltpu.VMEM),
    )


def activate_kernel(parts_ref, bias_ref, out_ref):
    hidden = bias_ref.shape[1]
    total = parts_ref[0].astype(f32)
    for k in range(1, parts_ref.shape[0]):
        total = total + parts_ref[k].astype(f32)
    pre = total[:, :hidden] + bias_ref[...]
    back = total[:, hidden:]
    square = pre * pre
    inner = jnp.tanh(root_coef * (pre + cube_coef * square * pre))
    half = 0.5 * (1.0 + inner)
    slope = half + 0.5 * pre * (1.0 - inner * inner) * root_coef * (
        1.0 + 3.0 * cube_coef * square
    )
    d_pre = (back * slope).astype(bf16)
    activ = (pre * half).astype(bf16)
    for k in range(out_ref.shape[0]):
        out_ref[k, 0] = d_pre
        out_ref[k, 1] = activ


def activate(parts, up_bias):
    quarters, rows, hidden = parts.shape[0], parts.shape[1], parts.shape[2] // 2
    return pl.pallas_call(
        activate_kernel,
        out_shape=jax.ShapeDtypeStruct((quarters, 2, rows, hidden), bf16),
        compiler_params=pltpu.CompilerParams(vmem_limit_bytes=VMEM),
        cost_estimate=cost(32 * parts.size, 4 * parts.size),
        name="activate",
    )(parts, up_bias)


def input_kernel(d_ref, up_ref, out_ref):
    out_ref[...] = lax.dot_general(
        d_ref[...], up_ref[...], (((1,), (1,)), ((), ())), preferred_element_type=f32
    ).astype(bf16)


def input_product(d_pre, up_weight):
    width, hidden = up_weight.shape
    steps = 2
    rows = d_pre.shape[0] // steps
    return pl.pallas_call(
        input_kernel,
        grid=(steps,),
        in_specs=[
            pl.BlockSpec((rows, hidden), lambda i: (i, 0)),
            pl.BlockSpec((width, hidden), lambda i: (0, 0)),
        ],
        out_specs=pl.BlockSpec((rows, width), lambda i: (i, 0)),
        out_shape=jax.ShapeDtypeStruct((steps * rows, width), bf16),
        compiler_params=pltpu.CompilerParams(vmem_limit_bytes=VMEM),
        cost_estimate=cost(2 * steps * rows * width * hidden, 2 * width * (steps * rows + hidden)),
        name="input_product",
    )(d_pre, up_weight)


def across(a, b):
    return lax.dot_general(a, b, (((0,), (0,)), ((), ())), preferred_element_type=f32)


def weights_kernel(
    factor, both_ref, d_ref, activ_ref, up_hbm, bias_ref, down_hbm, up_ref, down_ref, sems
):
    width, hidden = up_ref.shape
    steps = sems.shape[1]
    copies = []
    for k in range(steps):
        part = pl.ds(k * (width // steps), width // steps)
        up_ref[part, :] = (across(both_ref[:, part], d_ref[...]) * factor).astype(bf16)
        copies.append(pltpu.make_async_copy(up_ref.at[part], up_hbm.at[part], sems.at[0, k]))
        copies[-1].start()
    bias_ref[...] = jnp.sum(d_ref[...].astype(f32), axis=0, keepdims=True) * factor
    for k in range(steps):
        part = pl.ds(k * (hidden // steps), hidden // steps)
        down = across(activ_ref[:, part], both_ref[:, width:])
        down_ref[part, :] = (down * factor).astype(bf16)
        copies.append(pltpu.make_async_copy(down_ref.at[part], down_hbm.at[part], sems.at[1, k]))
        copies[-1].start()
    for copy in copies:
        copy.wait()


def weights_product(factor, both, d_pre, activ):
    tokens, width = both.shape[0], both.shape[1] // 2
    hidden = d_pre.shape[1]
    vmem = pl.BlockSpec(memory_space=pltpu.VMEM)
    hbm = pl.BlockSpec(memory_space=pltpu.HBM)
    return pl.pallas_call(
        functools.partial(weights_kernel, factor),
        in_specs=[vmem] * 3,
        out_specs=[hbm, vmem, hbm],
        out_shape=[
            pltpu.HBM((width, hidden), bf16),
            jax.ShapeDtypeStruct((1, hidden), f32),
            pltpu.HBM((hidden, width), bf16),
        ],
        scratch_shapes=[
            pltpu.VMEM((width, hidden), bf16),
            pltpu.VMEM((hidden, width), bf16),
            pltpu.SemaphoreType.DMA((2, 4)),
        ],
        compiler_params=pltpu.CompilerParams(vmem_limit_bytes=VMEM),
        cost_estimate=cost(4 * tokens * width * hidden, 4 * (tokens * width + width * hidden)),
        name="weights_product",
    )(both, d_pre, activ)


def spread(block, axes):
    copies = jnp.broadcast_to(block[None], (lax.axis_size(axes),) + block.shape)
    return lax.all_to_all(copies, axes, 0, 0)


def sum_kernel(parts_ref, out_ref):
    total = parts_ref[0].astype(f32)
    for k in range(1, parts_ref.shape[0]):
        total = total + parts_ref[k].astype(f32)
    out_ref[...] = total.astype(bf16)


def sum_parts(parts):
    vmem = pl.BlockSpec(memory_space=pltpu.VMEM)
    return pl.pallas_call(
        sum_kernel,
        in_specs=[vmem],
        out_specs=vmem,
        out_shape=jax.ShapeDtypeStruct(parts.shape[1:], bf16),
        compiler_params=pltpu.CompilerParams(vmem_limit_bytes=VMEM),
        cost_estimate=cost(parts.size, 2 * parts.size),
        name="sum_parts",
    )(pltpu.with_memory_space_constraint(parts, pltpu.VMEM))


def swap(block):
    return lax.ppermute(block, "core", [(0, 1), (1, 0)])


def shards(layer_input, up_weight, up_bias, down_weight, grad_output):
    tokens_here, width = layer_input.shape
    hidden = up_weight.shape[1]
    tokens = tokens_here * lax.axis_size(WIDE)
    factor = 1.0 / math.sqrt(tokens)
    core = lax.axis_index("core").astype(jnp.int32)[None]
    quarters = lax.axis_size("yh")

    both = jnp.concatenate([layer_input, grad_output], axis=1)
    both, core = lax.optimization_barrier((both, core))
    both = spread(both, "z").reshape(-1, 2 * width)
    both = spread(both, NEAR).reshape(-1, 2 * width)

    send, keep = forward(core, both, up_weight, down_weight)
    chip = (keep + swap(send).astype(f32)).astype(bf16)
    sums = lax.all_to_all(chip.reshape(quarters, -1, 2 * hidden), "yh", 0, 0)
    copies = activate(sums, up_bias[None])
    own = lax.all_to_all(copies, "yh", 0, 0)
    d_pre = lax.all_gather(own[:, 0].reshape(-1, hidden), "core", axis=0, tiled=True)
    partial = input_product(d_pre, up_weight)
    near = lax.axis_size(NEAR)
    parts = lax.all_to_all(partial.reshape(near, -1, width), NEAR, 0, 0)
    ends = sum_parts(parts)
    activ = lax.all_gather(own[:, 1].reshape(-1, hidden), "core", axis=0, tiled=True)
    up_grad, bias_grad, down_grad = weights_product(factor, both, d_pre, activ)
    ends = lax.all_to_all(ends.reshape(-1, tokens_here, width), "z", 0, 0)
    input_grad = jnp.sum(ends.astype(f32), axis=0).astype(bf16)
    return (input_grad, up_grad, bias_grad[0], down_grad)


def solution(mesh):
    fine = Mesh(mesh.devices.reshape(SIZES), AXES)
    in_specs = (
        P(WIDE, NARROW),
        P(NARROW, WIDE),
        P(WIDE),
        P(WIDE, NARROW),
        P(WIDE, NARROW),
    )
    out_specs = (P(WIDE, NARROW), P(NARROW, WIDE), P(WIDE), P(WIDE, NARROW))
    return jax.shard_map(shards, mesh=fine, in_specs=in_specs, out_specs=out_specs, check_vma=False)
```

```python
import functools
import math

import jax
import jax.numpy as jnp
from jax import lax
from jax.experimental import pallas as pl
from jax.experimental.pallas import tpu as pltpu
from jax.sharding import Mesh, PartitionSpec as P

AXES = ("z", "x", "yl", "yh", "core")
SIZES = (8, 4, 2, 4, 2)
NEAR = ("x", "yl")
WIDE = ("z", "x", "yl")
NARROW = ("yh", "core")

root_coef = 0.7978845608
cube_coef = 0.044715
f32 = jnp.float32
bf16 = jnp.bfloat16
VMEM = 16 * 1024 * 1024


def cost(flops, moved):
    return pl.CostEstimate(flops=flops, bytes_accessed=moved, transcendentals=0)


def forward_kernel(core_ref, both_ref, up_ref, down_ref, send_ref, keep_ref):
    rows, hidden = send_ref.shape[0], up_ref.shape[1]
    width = up_ref.shape[0]
    keep_at = pl.multiple_of(core_ref[0] * rows, rows)
    send_at = pl.multiple_of((1 - core_ref[0]) * rows, rows)

    def pre(start):
        x = both_ref[pl.ds(start, rows), :width]
        return jnp.dot(x, up_ref[...], preferred_element_type=f32)

    def back(start):
        g = both_ref[pl.ds(start, rows), width:]
        return lax.dot_general(
            g, down_ref[...], (((1,), (1,)), ((), ())), preferred_element_type=f32
        )

    send_ref[:, :hidden] = pre(send_at).astype(bf16)
    send_ref[:, hidden:] = back(send_at).astype(bf16)
    keep_ref[:, :hidden] = pre(keep_at)
    keep_ref[:, hidden:] = back(keep_at)


def forward(core, both, up_weight, down_weight):
    tokens, width = both.shape[0], both.shape[1] // 2
    hidden = up_weight.shape[1]
    rows = tokens // 2
    vmem = pl.BlockSpec(memory_space=pltpu.VMEM)
    return pl.pallas_call(
        forward_kernel,
        in_specs=[pl.BlockSpec(memory_space=pltpu.SMEM), vmem, vmem, vmem],
        out_specs=[vmem, vmem],
        out_shape=[
            jax.ShapeDtypeStruct((rows, 2 * hidden), bf16),
            jax.ShapeDtypeStruct((rows, 2 * hidden), f32),
        ],
        compiler_params=pltpu.CompilerParams(vmem_limit_bytes=VMEM),
        cost_estimate=cost(4 * tokens * width * hidden, 4 * (tokens * width + width * hidden)),
        name="forward_products",
    )(
        core,
        both,
        pltpu.with_memory_space_constraint(up_weight, pltpu.VMEM),
        pltpu.with_memory_space_constraint(down_weight, pltpu.VMEM),
    )


def activate_kernel(parts_ref, bias_ref, out_ref):
    hidden = bias_ref.shape[1]
    total = parts_ref[0].astype(f32)
    for k in range(1, parts_ref.shape[0]):
        total = total + parts_ref[k].astype(f32)
    pre = total[:, :hidden] + bias_ref[...]
    back = total[:, hidden:]
    square = pre * pre
    inner = jnp.tanh(root_coef * (pre + cube_coef * square * pre))
    half = 0.5 * (1.0 + inner)
    slope = half + 0.5 * pre * (1.0 - inner * inner) * root_coef * (
        1.0 + 3.0 * cube_coef * square
    )
    d_pre = (back * slope).astype(bf16)
    activ = (pre * half).astype(bf16)
    for k in range(out_ref.shape[0]):
        out_ref[k, 0] = d_pre
        out_ref[k, 1] = activ


def activate(parts, up_bias):
    quarters, rows, hidden = parts.shape[0], parts.shape[1], parts.shape[2] // 2
    return pl.pallas_call(
        activate_kernel,
        out_shape=jax.ShapeDtypeStruct((quarters, 2, rows, hidden), bf16),
        compiler_params=pltpu.CompilerParams(vmem_limit_bytes=VMEM),
        cost_estimate=cost(32 * parts.size, 4 * parts.size),
        name="activate",
    )(parts, up_bias)


def input_kernel(d_ref, up_ref, out_ref):
    out_ref[...] = lax.dot_general(
        d_ref[...], up_ref[...], (((1,), (1,)), ((), ())), preferred_element_type=f32
    ).astype(bf16)


def input_product(d_pre, up_weight):
    width, hidden = up_weight.shape
    steps = 2
    rows = d_pre.shape[0] // steps
    return pl.pallas_call(
        input_kernel,
        grid=(steps,),
        in_specs=[
            pl.BlockSpec((rows, hidden), lambda i: (i, 0)),
            pl.BlockSpec((width, hidden), lambda i: (0, 0)),
        ],
        out_specs=pl.BlockSpec((rows, width), lambda i: (i, 0)),
        out_shape=jax.ShapeDtypeStruct((steps * rows, width), bf16),
        compiler_params=pltpu.CompilerParams(vmem_limit_bytes=VMEM),
        cost_estimate=cost(2 * steps * rows * width * hidden, 2 * width * (steps * rows + hidden)),
        name="input_product",
    )(d_pre, up_weight)


def across(a, b):
    return lax.dot_general(a, b, (((0,), (0,)), ((), ())), preferred_element_type=f32)


def up_kernel(factor, both_ref, d_ref, up_hbm, bias_ref, up_ref, sems):
    steps = sems.shape[0]
    copies = []
    for k in range(steps):
        part = pl.ds(k * (up_ref.shape[0] // steps), up_ref.shape[0] // steps)
        up_ref[part, :] = (across(both_ref[:, part], d_ref[...]) * factor).astype(bf16)
        copies.append(pltpu.make_async_copy(up_ref.at[part], up_hbm.at[part], sems.at[k]))
        copies[-1].start()
    bias_ref[...] = jnp.sum(d_ref[...].astype(f32), axis=0, keepdims=True) * factor
    for copy in copies:
        copy.wait()


def down_kernel(factor, core_ref, both_ref, own_ref, other_ref, down_hbm, down_ref, sems):
    steps = sems.shape[0]
    hidden, width = down_ref.shape
    rows = own_ref.shape[0]
    mine = both_ref[pl.ds(pl.multiple_of(core_ref[0] * rows, rows), rows), width:]
    theirs = both_ref[pl.ds(pl.multiple_of((1 - core_ref[0]) * rows, rows), rows), width:]
    copies = []
    for k in range(steps):
        part = pl.ds(k * (hidden // steps), hidden // steps)
        down = across(own_ref[:, part], mine) + across(other_ref[:, part], theirs)
        down_ref[part, :] = (down * factor).astype(bf16)
        copies.append(pltpu.make_async_copy(down_ref.at[part], down_hbm.at[part], sems.at[k]))
        copies[-1].start()
    for copy in copies:
        copy.wait()


def up_product(factor, both, d_pre):
    tokens, width = both.shape[0], both.shape[1] // 2
    hidden = d_pre.shape[1]
    vmem = pl.BlockSpec(memory_space=pltpu.VMEM)
    return pl.pallas_call(
        functools.partial(up_kernel, factor),
        in_specs=[vmem] * 2,
        out_specs=[pl.BlockSpec(memory_space=pltpu.HBM), vmem],
        out_shape=[
            pltpu.HBM((width, hidden), bf16),
            jax.ShapeDtypeStruct((1, hidden), f32),
        ],
        scratch_shapes=[pltpu.VMEM((width, hidden), bf16), pltpu.SemaphoreType.DMA((4,))],
        compiler_params=pltpu.CompilerParams(vmem_limit_bytes=VMEM),
        cost_estimate=cost(2 * tokens * width * hidden, 2 * (tokens * width + width * hidden)),
        name="up_product",
    )(both, d_pre)


def down_product(factor, core, both, own, other):
    tokens, width = both.shape[0], both.shape[1] // 2
    hidden = own.shape[1]
    vmem = pl.BlockSpec(memory_space=pltpu.VMEM)
    return pl.pallas_call(
        functools.partial(down_kernel, factor),
        in_specs=[pl.BlockSpec(memory_space=pltpu.SMEM)] + [vmem] * 3,
        out_specs=pl.BlockSpec(memory_space=pltpu.HBM),
        out_shape=pltpu.HBM((hidden, width), bf16),
        scratch_shapes=[pltpu.VMEM((hidden, width), bf16), pltpu.SemaphoreType.DMA((4,))],
        compiler_params=pltpu.CompilerParams(vmem_limit_bytes=VMEM),
        cost_estimate=cost(2 * tokens * width * hidden, 2 * (tokens * width + width * hidden)),
        name="down_product",
    )(core, both, own, other)


def spread(block, axes):
    copies = jnp.broadcast_to(block[None], (lax.axis_size(axes),) + block.shape)
    return lax.all_to_all(copies, axes, 0, 0)


def sum_kernel(parts_ref, out_ref):
    total = parts_ref[0].astype(f32)
    for k in range(1, parts_ref.shape[0]):
        total = total + parts_ref[k].astype(f32)
    out_ref[...] = total.astype(bf16)


def sum_parts(parts):
    vmem = pl.BlockSpec(memory_space=pltpu.VMEM)
    return pl.pallas_call(
        sum_kernel,
        in_specs=[vmem],
        out_specs=vmem,
        out_shape=jax.ShapeDtypeStruct(parts.shape[1:], bf16),
        compiler_params=pltpu.CompilerParams(vmem_limit_bytes=VMEM),
        cost_estimate=cost(parts.size, 2 * parts.size),
        name="sum_parts",
    )(pltpu.with_memory_space_constraint(parts, pltpu.VMEM))


def swap(block):
    return lax.ppermute(block, "core", [(0, 1), (1, 0)])


def shards(layer_input, up_weight, up_bias, down_weight, grad_output):
    tokens_here, width = layer_input.shape
    hidden = up_weight.shape[1]
    tokens = tokens_here * lax.axis_size(WIDE)
    factor = 1.0 / math.sqrt(tokens)
    core = lax.axis_index("core").astype(jnp.int32)[None]
    quarters = lax.axis_size("yh")

    both = jnp.concatenate([layer_input, grad_output], axis=1)
    both, core = lax.optimization_barrier((both, core))
    both = spread(both, "z").reshape(-1, 2 * width)
    both = spread(both, NEAR).reshape(-1, 2 * width)

    send, keep = forward(core, both, up_weight, down_weight)
    chip = (keep + swap(send).astype(f32)).astype(bf16)
    sums = lax.all_to_all(chip.reshape(quarters, -1, 2 * hidden), "yh", 0, 0)
    copies = activate(sums, up_bias[None])
    own = lax.all_to_all(copies, "yh", 0, 0)
    d_pre = lax.all_gather(own[:, 0].reshape(-1, hidden), "core", axis=0, tiled=True)
    partial = input_product(d_pre, up_weight)
    near = lax.axis_size(NEAR)
    parts = lax.all_to_all(partial.reshape(near, -1, width), NEAR, 0, 0)
    ends = sum_parts(parts)
    ends, activ = lax.optimization_barrier((ends, own[:, 1].reshape(-1, hidden)))
    up_grad, bias_grad = up_product(factor, both, d_pre)
    down_grad = down_product(factor, core, both, activ, swap(activ))
    ends = lax.all_to_all(ends.reshape(-1, tokens_here, width), "z", 0, 0)
    input_grad = jnp.sum(ends.astype(f32), axis=0).astype(bf16)
    return (input_grad, up_grad, bias_grad[0], down_grad)


def solution(mesh):
    fine = Mesh(mesh.devices.reshape(SIZES), AXES)
    in_specs = (
        P(WIDE, NARROW),
        P(NARROW, WIDE),
        P(WIDE),
        P(WIDE, NARROW),
        P(WIDE, NARROW),
    )
    out_specs = (P(WIDE, NARROW), P(NARROW, WIDE), P(WIDE), P(WIDE, NARROW))
    return jax.shard_map(shards, mesh=fine, in_specs=in_specs, out_specs=out_specs, check_vma=False)
```
